256 devices in a mesh: section: 8 (over z_lo, x), dp: 32 (over z_hi, y, core).
Axes of the slice: x: 4, y: 4, z: 8 (z_hi: 4, z_lo: 2; z = z_hi * 2 + z_lo), core: 2. Of those that a mesh axis runs over, the one named last changes fastest.
Arguments:
- novel_batch_seq: bfloat16 [3, 256, 1024], P(None, 'dp'), may hold values from -6 to 6
- transit_activity: bfloat16 [8, 256, 1024], P('section', 'dp'), may hold values from -6 to 6
- saved_prior_entries: bfloat16 [8, 14, 256, 1024], P('section', None, 'dp'), may hold values from -6 to 6
- waiting_loss_slope: bfloat16 [8, 256, 1024], P('section', 'dp'), may hold values from -4 to 4
- loss_slope_seq: bfloat16 [3, 256, 1024], P(None, 'dp'), may hold values from -4 to 4
- norm_scaling: float32 [8, 1024], P('section'), may hold values from 0.5 to 2
- entering_matrix: bfloat16 [8, 1024, 32768], P('section', None, 'dp'), may hold values from -0.1875 to 0.1875
- leaving_matrix: bfloat16 [8, 32768, 1024], P('section', 'dp'), may hold values from -0.03125 to 0.03125
Outputs:
- activations: bfloat16 [8, 3, 256, 1024], P('section', None, 'dp')
- input_grads: bfloat16 [8, 3, 256, 1024], P('section', None, 'dp')
- grad_w_in: bfloat16 [8, 1024, 32768], P('section', None, 'dp')
- grad_w_out: bfloat16 [8, 32768, 1024], P('section', 'dp')
- grad_gain: float32 [8, 1024], P('section')
The draws below stay inside these ranges and needn't reach their ends.
All inputs are finite; a program needn't handle non-finite values.
Results may differ from the reference program's by a relative error of at most 0.023.
Values may be sent and summed in bfloat16 or wider, within the bound.
No kernel may reach another device: no remote copies, remote signals or barrier semaphores. Data moves between devices by JAX's collectives and lax.ppermute only.
A program may use at most 128 MiB of HBM per device.

```python
import math
import jax
import jax.numpy as jnp
from jax import lax

HIDDEN_DIM = 1024
FF = 32768
SMALL_BATCH_LEN = 256
TICKS = 3
LAYER_PARTS = 8
DEPTH = 14


def block_scale(own_key, dims, pieces, low, high):
    level = 1.0
    for axis_at, shards_of in pieces:
        draws = jax.random.uniform(jax.random.fold_in(jax.random.fold_in(own_key, 6), axis_at), (shards_of,), jnp.float32, low / len(pieces), high / len(pieces))
        level = level * jnp.repeat(jnp.exp(draws), dims[axis_at] // shards_of).reshape((-1,) + (1,) * (len(dims) - 1 - axis_at))
    return level


def noise(key, shape, width, most, cuts=(), held_as=jnp.bfloat16):
    level = block_scale(key, shape, cuts, -0.22, 0.18) if cuts else 1.0
    array = jax.random.normal(key, shape, jnp.float32) * width * level
    return jnp.minimum(jnp.maximum(array, -most), most).astype(held_as)


def setup_inputs(seed: int = 0) -> dict:
    key_of = jax.random.split(jax.random.key(seed), 9)
    novel_batch_seq = noise(key_of[0], (TICKS, SMALL_BATCH_LEN, HIDDEN_DIM), 1.0, 6.0, ((1, 32),))
    transit_activity = noise(key_of[1], (LAYER_PARTS, SMALL_BATCH_LEN, HIDDEN_DIM), 1.0, 6.0, ((0, 8), (1, 32)))
    saved_prior_entries = noise(key_of[2], (LAYER_PARTS, DEPTH, SMALL_BATCH_LEN, HIDDEN_DIM), 1.0, 6.0, ((0, 8), (2, 32)))
    waiting_loss_slope = noise(key_of[3], (LAYER_PARTS, SMALL_BATCH_LEN, HIDDEN_DIM), 0.25, 4.0, ((0, 8), (1, 32)))
    loss_slope_seq = noise(key_of[4], (TICKS, SMALL_BATCH_LEN, HIDDEN_DIM), 0.25, 4.0, ((1, 32),))
    norm_scaling = jnp.clip(jnp.exp(math.log(2.0) - 1.3862944 * jax.random.uniform(key_of[5], (LAYER_PARTS, HIDDEN_DIM), jnp.float32) ** block_scale(key_of[5], (LAYER_PARTS, HIDDEN_DIM), ((0, 8),), -0.2, 0.2)), 0.5, 2.0)
    entering_matrix = noise(key_of[6], (LAYER_PARTS, HIDDEN_DIM, FF), HIDDEN_DIM ** -0.5, 0.1875, ((0, 8), (2, 32)))
    leaving_matrix = noise(key_of[7], (LAYER_PARTS, FF, HIDDEN_DIM), FF ** -0.5, 0.03125, ((0, 8), (1, 32)))
    return {"novel_batch_seq": novel_batch_seq, "transit_activity": transit_activity, "saved_prior_entries": saved_prior_entries, "waiting_loss_slope": waiting_loss_slope, "loss_slope_seq": loss_slope_seq, "norm_scaling": norm_scaling, "entering_matrix": entering_matrix, "leaving_matrix": leaving_matrix}


gelu_coef = 0.7978845608028654
gelu_cubic = 0.044715
norm_eps = 1e-06

def gelu_value(pre_act):
    inner = gelu_coef * (pre_act + gelu_cubic * pre_act * pre_act * pre_act)
    return 0.5 * pre_act * (1.0 + jnp.tanh(inner))

def gelu_slope(pre_act):
    tangent = jnp.tanh(gelu_coef * (pre_act + gelu_cubic * pre_act * pre_act * pre_act))
    return 0.5 * (1.0 + tangent) + 0.5 * pre_act * (1.0 - tangent * tangent) * gelu_coef * (1.0 + 3.0 * gelu_cubic * pre_act * pre_act)

def normalize(rows_in, gain_row):
    widened = rows_in.astype(jnp.float32)
    factor = lax.rsqrt(lax.optimization_barrier(jnp.mean(widened * widened, axis=-1, keepdims=True)) + norm_eps)
    return ((widened * factor * gain_row).astype(jnp.bfloat16), widened, factor)

def section_forward(rows_in, gain_row, weight_in, weight_out):
    normed, widened, factor = normalize(rows_in, gain_row)
    hidden = gelu_value(jnp.dot(normed, weight_in, preferred_element_type=jnp.float32)).astype(jnp.bfloat16)
    total = jnp.dot(hidden, weight_out, preferred_element_type=jnp.float32)
    return (widened + total).astype(jnp.bfloat16)

def section_backward(rows_in, grad_rows, gain_row, weight_in, weight_out):
    normed, widened, factor = normalize(rows_in, gain_row)
    pre_act = jnp.dot(normed, weight_in, preferred_element_type=jnp.float32)
    hidden = gelu_value(pre_act).astype(jnp.bfloat16)
    grad_out = jnp.dot(hidden.T, grad_rows, preferred_element_type=jnp.float32)
    grad_hidden = jnp.dot(grad_rows, weight_out.T, preferred_element_type=jnp.float32)
    grad_pre = (grad_hidden * gelu_slope(pre_act)).astype(jnp.bfloat16)
    grad_in = jnp.dot(normed.T, grad_pre, preferred_element_type=jnp.float32)
    grad_normed = jnp.dot(grad_pre, weight_in.T, preferred_element_type=jnp.float32)
    weighted = gain_row * grad_normed
    inner = lax.optimization_barrier(jnp.mean(weighted * widened, axis=-1, keepdims=True))
    grad_x = grad_rows.astype(jnp.float32) + factor * weighted - widened * (factor * factor * factor) * inner
    gain_term = lax.optimization_barrier(jnp.sum(grad_normed * widened * factor, axis=0))
    return (grad_x.astype(jnp.bfloat16), grad_in, grad_out, gain_term)

def reference(novel_batch_seq, transit_activity, saved_prior_entries, waiting_loss_slope, loss_slope_seq, norm_scaling, entering_matrix, leaving_matrix):
    forward_inputs = []
    activations = []
    for segment_update in range(LAYER_PARTS):
        inputs_here = []
        outputs_here = []
        for tick in range(TICKS):
            if segment_update == 0:
                present_entry_vector = novel_batch_seq[tick]
            elif tick == 0:
                present_entry_vector = transit_activity[segment_update]
            else:
                present_entry_vector = activations[segment_update - 1][tick - 1]
            inputs_here.append(present_entry_vector)
            outputs_here.append(section_forward(present_entry_vector, norm_scaling[segment_update], entering_matrix[segment_update], leaving_matrix[segment_update]))
        forward_inputs.append(inputs_here)
        activations.append(outputs_here)
    input_grads = [None] * LAYER_PARTS
    grads_in = [None] * LAYER_PARTS
    grads_out = [None] * LAYER_PARTS
    grads_gain = [None] * LAYER_PARTS
    for segment_update in reversed(range(LAYER_PARTS)):
        acc_in = jnp.zeros(entering_matrix.shape[1:], jnp.float32)
        acc_out = jnp.zeros(leaving_matrix.shape[1:], jnp.float32)
        acc_gain = jnp.zeros(norm_scaling.shape[1:], jnp.float32)
        grads_here = []
        for tick in range(TICKS):
            source_tick = tick - 2 * (LAYER_PARTS - 1 - segment_update)
            if source_tick >= 0:
                x_back = forward_inputs[segment_update][source_tick]
            else:
                x_back = saved_prior_entries[segment_update, tick + 2 * segment_update]
            if segment_update == LAYER_PARTS - 1:
                gradient_current = loss_slope_seq[tick]
            elif tick == 0:
                gradient_current = waiting_loss_slope[segment_update]
            else:
                gradient_current = input_grads[segment_update + 1][tick - 1]
            grad_x, grad_in, grad_out, gain_term = section_backward(x_back, gradient_current, norm_scaling[segment_update], entering_matrix[segment_update], leaving_matrix[segment_update])
            acc_in = acc_in + grad_in
            acc_out = acc_out + grad_out
            acc_gain = acc_gain + gain_term
            grads_here.append(grad_x)
        input_grads[segment_update] = grads_here
        grads_in[segment_update] = acc_in.astype(jnp.bfloat16)
        grads_out[segment_update] = acc_out.astype(jnp.bfloat16)
        grads_gain[segment_update] = acc_gain
    act_out = jnp.stack([jnp.stack(row) for row in activations])
    grad_rows_out = jnp.stack([jnp.stack(row) for row in input_grads])
    return (act_out, grad_rows_out, jnp.stack(grads_in), jnp.stack(grads_out), jnp.stack(grads_gain))
```

```python
import jax
import jax.numpy as jnp
from jax import lax
from jax.sharding import PartitionSpec as P

gelu_coef = 0.7978845608028654
gelu_cubic = 0.044715
norm_eps = 1e-06
bf16 = jnp.bfloat16
f32 = jnp.float32

Z, Y, CORES = 4, 4, 2


def place(index):
    return index // (Y * CORES), index // CORES % Y, index % CORES


def route(value, dz, dy, dc):
    pairs = []
    for i in range(Z * Y * CORES):
        z, y, c = place(i)
        pairs.append((i, ((z + dz) % Z * Y + (y + dy) % Y) * CORES + (c ^ dc)))
    return lax.ppermute(value, "dp", pairs)


def shifted(value, axis, by):
    devices = lax.axis_size(axis)
    pairs = [(i, i + by) for i in range(devices) if 0 <= i + by < devices]
    return lax.ppermute(value, axis, pairs)


def gather_z(rows):
    return jnp.concatenate([rows] + [route(rows, -k, 0, 0) for k in range(1, Z)], axis=-2)


def gather_yc(rows):
    rows = jnp.concatenate([rows] + [route(rows, 0, -k, 0) for k in range(1, Y)], axis=-2)
    return jnp.concatenate([rows, route(rows, 0, 0, 1)], axis=-2)


def reduce_cy(part, extra=None):
    half = part.shape[0] // CORES
    block = half // Y

    def pack(rows):
        rows = rows.astype(bf16)
        return rows if extra is None else jnp.concatenate([rows, extra.astype(bf16)], axis=0)

    def unpack(rows, size):
        rows = rows.astype(f32)
        return rows[:size], (None if extra is None else rows[size:])

    got, more = unpack(route(pack(part[half:]), 0, 0, 1), half)
    part = part[:half] + got
    if extra is not None:
        extra = extra + more
    total, sent = part[:block], extra
    arrived = [route(pack(part[block * k : block * (k + 1)]), 0, k, 0) for k in range(1, Y)]
    for rows in arrived:
        got, more = unpack(rows, block)
        total = total + got
        if extra is not None:
            sent = sent + more
    return total, sent


def reduce_z_all(total):
    rows = total.shape[0] // Z
    narrow = total.astype(bf16)
    for k in range(1, Z):
        got = route(narrow, k, 0, 0).astype(f32)
        total = total + jnp.concatenate([got[rows * k :], got[: rows * k]], axis=0)
    return total


def reduce_z_own(total, extra=None):
    rows = total.shape[0] // Z
    own = total[:rows]
    for k in range(1, Z):
        piece = total[rows * k : rows * (k + 1)].astype(bf16)
        if extra is not None:
            piece = jnp.concatenate([piece, extra.astype(bf16)], axis=0)
        got = route(piece, k, 0, 0).astype(f32)
        own = own + got[:rows]
        if extra is not None:
            grown = got[rows:] if k == 1 else grown + got[rows:]
    return own, (None if extra is None else extra + grown)


def gelu_value(pre_act):
    inner = gelu_coef * (pre_act + gelu_cubic * pre_act * pre_act * pre_act)
    return 0.5 * pre_act * (1.0 + jnp.tanh(inner))


def gelu_slope(pre_act):
    tangent = jnp.tanh(gelu_coef * (pre_act + gelu_cubic * pre_act * pre_act * pre_act))
    return 0.5 * (1.0 + tangent) + 0.5 * pre_act * (1.0 - tangent * tangent) * gelu_coef * (
        1.0 + 3.0 * gelu_cubic * pre_act * pre_act
    )


def normalize(rows_in, gain_row):
    widened = rows_in.astype(f32)
    factor = lax.rsqrt(jnp.mean(widened * widened, axis=-1, keepdims=True) + norm_eps)
    return ((widened * factor * gain_row).astype(bf16), widened, factor)


def dot(a, b, ca, cb):
    return lax.dot_general(a, b, (((ca,), (cb,)), ((), ())), preferred_element_type=f32)


def norm_backward(rows, factor, grad_normed, grad_rows, gain_row):
    weighted = gain_row * grad_normed
    inner = jnp.mean(weighted * rows, axis=-1, keepdims=True)
    grad_x = grad_rows.astype(f32) + factor * weighted - rows * (factor * factor * factor) * inner
    return grad_x.astype(bf16)


def on_device(
    novel_batch_seq,
    transit_activity,
    saved_prior_entries,
    waiting_loss_slope,
    loss_slope_seq,
    norm_scaling,
    entering_matrix,
    leaving_matrix,
):
    section_pos = lax.axis_index("section")
    section_count = lax.axis_size("section")
    ticks, own_rows = novel_batch_seq.shape[:2]
    depth = saved_prior_entries.shape[1]
    gain_row = norm_scaling[0]
    weight_in = entering_matrix[0]
    weight_out = leaving_matrix[0]
    is_first = section_pos == 0
    is_last = section_pos == section_count - 1
    x_first = jnp.where(is_first, novel_batch_seq[0], transit_activity[0])
    g_first = jnp.where(is_last, loss_slope_seq[0], waiting_loss_slope[0])
    history = jnp.concatenate([saved_prior_entries[0], x_first[None]], axis=0)
    stored = [
        lax.dynamic_index_in_dim(
            history, jnp.minimum(tick + 2 * section_pos, depth), 0, keepdims=False
        )
        for tick in range(ticks)
    ]
    entering = jnp.stack(
        [jnp.where(is_last, loss_slope_seq[t], novel_batch_seq[t]) for t in range(1, ticks)]
    )
    x_all = gather_yc(gather_z(x_first))
    g_all, s_all = gather_yc(gather_z(jnp.stack([g_first, stored[0]])))
    later = gather_yc(gather_z(jnp.stack(stored[1:])))
    entering = gather_z(entering)
    near = own_rows * Z

    forward_outs, backward_outs = [], []
    normed_seq, hidden_seq, grad_pre_seq, slope_seq = [], [], [], []
    gain_part = jnp.zeros((8, gain_row.shape[0]), f32)
    for tick in range(ticks):
        final = tick + 1 == ticks
        normed, _, _ = normalize(x_all, gain_row)
        hidden = gelu_value(dot(normed, weight_in, 1, 0)).astype(bf16)
        total, _ = reduce_cy(dot(hidden, weight_out, 1, 0))
        if final:
            total, _ = reduce_z_own(total)
        else:
            total = reduce_z_all(total)
        y_now = (x_all[: total.shape[0]].astype(f32) + total).astype(bf16)
        forward_outs.append(y_now[:own_rows])

        if tick:
            s_all = jnp.where(is_last, x_all, later[tick - 1])
        normed_back, wide_back, factor_back = normalize(s_all, gain_row)
        pre_act = dot(normed_back, weight_in, 1, 0)
        hidden_seq.append(gelu_value(pre_act).astype(bf16))
        grad_pre = (dot(g_all, weight_out, 1, 1) * gelu_slope(pre_act)).astype(bf16)
        part = dot(grad_pre, weight_in, 1, 1)
        gain_part = gain_part + jnp.sum(
            (part * wide_back * factor_back).reshape(-1, 8, part.shape[1]), axis=0
        )
        normed_seq.append(normed_back)
        grad_pre_seq.append(grad_pre)
        slope_seq.append(g_all)
        if final:
            total, gain_part = reduce_z_own(*reduce_cy(part, gain_part))
        else:
            total = reduce_z_all(reduce_cy(part)[0])
        size = total.shape[0]
        grad_x = norm_backward(
            wide_back[:size], factor_back[:size], total, g_all[:size], gain_row
        )
        backward_outs.append(grad_x[:own_rows])
        if not final:
            x_all = gather_yc(jnp.where(is_first, entering[tick], shifted(y_now, "section", 1)))
            g_all = gather_yc(jnp.where(is_last, entering[tick], shifted(grad_x, "section", -1)))

    normed_seq, hidden_seq, grad_pre_seq, slope_seq = (
        jnp.concatenate(seq, axis=0) for seq in (normed_seq, hidden_seq, grad_pre_seq, slope_seq)
    )
    grad_in = dot(normed_seq, grad_pre_seq, 0, 0).astype(bf16)
    grad_out = dot(hidden_seq, slope_seq, 0, 0).astype(bf16)
    gain_total = jnp.sum(gain_part, axis=0)
    return (
        jnp.stack(forward_outs)[None],
        jnp.stack(backward_outs)[None],
        grad_in[None],
        grad_out[None],
        gain_total[None],
    )


def solution(mesh):
    placed = (
        P(None, "dp", None),
        P("section", "dp", None),
        P("section", None, "dp", None),
        P("section", "dp", None),
        P(None, "dp", None),
        P("section", None),
        P("section", None, "dp"),
        P("section", "dp", None),
    )
    return jax.shard_map(
        on_device,
        mesh=mesh,
        in_specs=placed,
        out_specs=(
            P("section", None, "dp", None),
            P("section", None, "dp", None),
            P("section", None, "dp"),
            P("section", "dp", None),
            P("section", None),
        ),
        check_vma=False,
    )
```

```python
import functools

import jax
import jax.numpy as jnp
from jax import lax
from jax.experimental import pallas as pl
from jax.experimental.pallas import tpu as pltpu
from jax.sharding import PartitionSpec as P

gelu_coef = 0.7978845608028654
gelu_cubic = 0.044715
norm_eps = 1e-06
bf16 = jnp.bfloat16
f32 = jnp.float32

Z, Y, CORES = 4, 4, 2
OWN = 8
NEAR = OWN * Z
HALF = NEAR * Y
WIDE = 1024
CHUNK = 256
MIB = 1024 * 1024


def place(index):
    return index // (Y * CORES), index // CORES % Y, index % CORES


def route(value, dz, dy, dc):
    pairs = []
    for i in range(Z * Y * CORES):
        z, y, c = place(i)
        pairs.append((i, ((z + dz) % Z * Y + (y + dy) % Y) * CORES + (c ^ dc)))
    return lax.ppermute(value, "dp", pairs)


def shifted(value, by):
    devices = lax.axis_size("section")
    pairs = [(i, i + by) for i in range(devices) if 0 <= i + by < devices]
    return lax.ppermute(value, "section", pairs)


def out(dtype, *shape):
    return jax.ShapeDtypeStruct(shape, dtype)


def local(body, outs, *operands, scalars=0, limit=8, scratch=(), flops=0):
    size = sum(math_size(o) for o in operands) + sum(math_size(o) for o in outs)
    specs = [pl.BlockSpec(memory_space=pltpu.SMEM)] * scalars
    specs += [pl.BlockSpec(memory_space=pltpu.VMEM)] * (len(operands) - scalars)
    return pl.pallas_call(
        body,
        out_shape=tuple(outs),
        in_specs=specs,
        out_specs=tuple([pl.BlockSpec(memory_space=pltpu.VMEM)] * len(outs)),
        scratch_shapes=list(scratch),
        compiler_params=pltpu.CompilerParams(vmem_limit_bytes=limit * MIB),
        cost_estimate=pl.CostEstimate(flops=flops, bytes_accessed=size, transcendentals=0),
    )(*operands)


def math_size(array):
    total = jnp.dtype(array.dtype).itemsize
    for d in array.shape:
        total *= d
    return total


def dot(a, b, ca, cb):
    return lax.dot_general(a, b, (((ca,), (cb,)), ((), ())), preferred_element_type=f32)


def rms_factor(wide):
    return lax.rsqrt(jnp.mean(wide * wide, axis=-1, keepdims=True) + norm_eps)


def tangent_of(pre_act):
    return jnp.tanh(gelu_coef * (pre_act + gelu_cubic * pre_act * pre_act * pre_act))


def tick_body(
    separate, flags, near, far, s_near, s_far, gain, w_in, w_out, gain_was,
    send, keep, normed_back, hidden_back, grad_pre, gain_sum,
    normed, hidden,
):
    is_last = flags[1]
    row = gain[...]
    for i, (half, s_half) in enumerate(((near, s_near), (far, s_far))):
        rows = pl.ds(i * HALF, HALF)
        x = half[0].astype(f32)
        normed[rows, :] = (x * rms_factor(x) * row).astype(bf16)
        x = s_half[...].astype(f32) if separate else jnp.where(
            is_last == 1, x, s_half[...].astype(f32)
        )
        value = (x * rms_factor(x) * row).astype(bf16)
        normed[pl.ds(2 * HALF + i * HALF, HALF), :] = value
        normed_back[rows, :] = value

    def first(step, carry):
        cols = pl.ds(pl.multiple_of(step * CHUNK, CHUNK), CHUNK)
        pre = dot(normed[: 2 * HALF, :], w_in[:, cols], 1, 0)
        hidden[:, cols] = (0.5 * pre * (1.0 + tangent_of(pre))).astype(bf16)
        for i, half in enumerate((near, far)):
            rows = pl.ds(i * HALF, HALF)
            pre = dot(normed[pl.ds(2 * HALF + i * HALF, HALF), :], w_in[:, cols], 1, 0)
            tangent = tangent_of(pre)
            hidden_back[rows, cols] = (0.5 * pre * (1.0 + tangent)).astype(bf16)
            slope = 0.5 * (1.0 + tangent) + 0.5 * pre * (1.0 - tangent * tangent) * gelu_coef * (
                1.0 + 3.0 * gelu_cubic * pre * pre
            )
            grad_hidden = dot(half[1], w_out[cols, :], 1, 1)
            grad_pre[rows, cols] = (grad_hidden * slope).astype(bf16)
        return carry

    lax.fori_loop(0, WIDE // CHUNK, first, 0)

    def second(step, carry):
        cols = pl.ds(pl.multiple_of(step * CHUNK, CHUNK), CHUNK)
        part = dot(hidden[...], w_out[:, cols], 1, 0)
        keep[0, :, cols] = part[:HALF]
        send[0, :, cols] = part[HALF:].astype(bf16)
        part = dot(grad_pre[...], w_in[cols, :], 1, 1)
        keep[1, :, cols] = part[:HALF]
        send[1, :, cols] = part[HALF:].astype(bf16)
        unit = normed_back[:, cols].astype(f32)
        term = jnp.sum((part * unit).reshape(-1, 8, CHUNK), axis=0)
        gain_sum[0, :, cols] = gain_was[0, :, cols] + term / gain[:, cols]
        return carry

    lax.fori_loop(0, WIDE // CHUNK, second, 0)


def split_body(passed, keep, arrived, *refs):
    total, blocks = refs[passed], refs[passed + 1 :]
    for j in range(Y):
        rows = slice(j * NEAR, (j + 1) * NEAR)
        value = keep[:, rows] + arrived[:, rows].astype(f32)
        if j == 0:
            total[...] = value
        else:
            blocks[j - 1][...] = value.astype(bf16)
    if passed:
        blocks[-1][...] = refs[0][...]


def stack_z(parts):
    return jnp.concatenate([p.astype(f32) for p in parts], axis=-2).astype(bf16)


def sum_body(passed, total, *refs):
    value = total[...]
    for r in refs[: Y - 1]:
        value = value + r[...].astype(f32)
    wide, narrow = refs[Y - 1 + passed : Y + 1 + passed]
    wide[...] = value
    narrow[...] = value.astype(bf16)
    if passed:
        later, entering = refs[Y + 1 + passed :]
        value = stack_z([r[...] for r in refs[Y - 1 : Y - 1 + passed]])
        later[...] = value[:2]
        entering[...] = value[2:]


def norm_backward(x, grad_normed, grad_rows, row):
    factor = rms_factor(x)
    weighted = row * grad_normed
    inner = jnp.mean(weighted * x, axis=-1, keepdims=True)
    return grad_rows + factor * weighted - x * (factor * factor * factor) * inner


def finish_body(separate, passed, flags, total, r1, r2, r3, near, s_near, gain, *refs):
    fwd, bwd = total[0], total[1]
    for k, ref in enumerate((r1, r2, r3)):
        turn = (k + 1) * OWN
        got = ref[0].astype(f32)
        fwd = fwd + jnp.concatenate([got[turn:], got[:turn]], axis=0)
        got = ref[1].astype(f32)
        bwd = bwd + jnp.concatenate([got[turn:], got[:turn]], axis=0)
    y_now, grad_x = refs[passed], refs[passed + 1]
    x = near[0, :NEAR].astype(f32)
    y_now[...] = (x + fwd).astype(bf16)
    x_back = s_near[:NEAR].astype(f32)
    if not separate:
        x_back = jnp.where(flags[1] == 1, x, x_back)
    grads = near[1, :NEAR].astype(f32)
    grad_x[...] = norm_backward(x_back, bwd, grads, gain[...]).astype(bf16)
    if passed:
        join(refs[:passed], refs[passed + 2])


def join(parts, whole):
    for j, part in enumerate(parts):
        whole[:, j * NEAR : (j + 1) * NEAR, :] = part[...]


def select_body(flags, y_in, g_in, entering, rows):
    rows[0] = jnp.where(flags[0] == 1, entering[...].astype(f32), y_in[...].astype(f32)).astype(bf16)
    rows[1] = jnp.where(flags[1] == 1, entering[...].astype(f32), g_in[...].astype(f32)).astype(bf16)


def join_body(*refs):
    join(refs[:-1], refs[-1])


def join_z_body(*refs):
    refs[-1][...] = stack_z([r[...] for r in refs[:-1]])


def gather_y(rows):
    parts = [rows] + [route(rows, 0, -j, 0) for j in range(1, Y)]
    return local(join_body, [out(bf16, rows.shape[0], HALF, WIDE)], *parts)[0]


def last_split_body(keep, arrived, gain_sum, gain_in, total, gain_total, *blocks):
    gain_value = gain_sum[...] + gain_in[...].astype(f32)
    gain_total[...] = gain_value
    for j in range(Y):
        rows = slice(j * NEAR, (j + 1) * NEAR)
        value = keep[:, rows] + arrived[:, rows].astype(f32)
        if j == 0:
            total[...] = value
        else:
            for i in range(2):
                for k in range(Z):
                    blocks[j - 1][i * Z + k] = value[i, k * OWN : (k + 1) * OWN].astype(bf16)
            blocks[j - 1][2 * Z] = gain_value[0].astype(bf16)


def last_sum_body(total, gain_total, r1, r2, r3, own, *blocks):
    gain_value = gain_total[0]
    for ref in (r1, r2, r3):
        gain_value = gain_value + ref[2 * Z].astype(f32)
    for k in range(Z):
        for i in range(2):
            value = total[i, k * OWN : (k + 1) * OWN]
            for ref in (r1, r2, r3):
                value = value + ref[i * Z + k].astype(f32)
            if k == 0:
                own[i] = value
            else:
                blocks[k - 1][i] = value.astype(bf16)
        if k == 0:
            own[2] = gain_value
        else:
            blocks[k - 1][2] = gain_value.astype(bf16)


def last_body(flags, own, r1, r2, r3, near, s_near, gain, y_now, grad_x, gain_total):
    fwd, bwd, gain_value = own[0], own[1], own[2]
    for ref in (r1, r2, r3):
        fwd = fwd + ref[0].astype(f32)
        bwd = bwd + ref[1].astype(f32)
        gain_value = gain_value + ref[2].astype(f32)
    x = near[0, :16].astype(f32)[:OWN]
    y_now[...] = (x + fwd).astype(bf16)
    x_back = jnp.where(flags[1] == 1, x, s_near[:16].astype(f32)[:OWN])
    grads = near[1, :16].astype(f32)[:OWN]
    grad_x[...] = norm_backward(x_back, bwd, grads, gain[...]).astype(bf16)
    gain_total[...] = jnp.sum(gain_value, axis=0, keepdims=True)


def on_device(
    novel_batch_seq,
    transit_activity,
    saved_prior_entries,
    waiting_loss_slope,
    loss_slope_seq,
    norm_scaling,
    entering_matrix,
    leaving_matrix,
):
    section_pos = lax.axis_index("section")
    section_count = lax.axis_size("section")
    ticks = novel_batch_seq.shape[0]
    depth = saved_prior_entries.shape[1]
    weight_in = entering_matrix[0]
    weight_out = leaving_matrix[0]
    is_first = section_pos == 0
    is_last = section_pos == section_count - 1
    flags = jnp.stack([is_first, is_last]).astype(jnp.int32)
    x_first = jnp.where(is_first, novel_batch_seq[0], transit_activity[0])
    g_first = jnp.where(is_last, loss_slope_seq[0], waiting_loss_slope[0])
    stored = []
    for tick in range(ticks):
        index = tick + 2 * section_pos
        held = lax.dynamic_index_in_dim(
            saved_prior_entries[0], jnp.minimum(index, depth - 1), 0, keepdims=False
        )
        stored.append(jnp.where(index < depth, held, x_first))
    entering = [jnp.where(is_last, loss_slope_seq[t], novel_batch_seq[t]) for t in range(1, ticks)]
    begin = jnp.stack([x_first, g_first, stored[0]])
    later = jnp.stack(stored[1:] + entering)

    parts = [begin] + [route(begin, -k, 0, 0) for k in range(1, Z)]
    near = gather_y(local(join_z_body, [out(bf16, 3, NEAR, WIDE)], *parts)[0])
    far = route(near, 0, 0, 1)
    s_near, s_far = near[2], far[2]

    block = (2, NEAR, WIDE)
    whole = (2 * HALF, WIDE)
    gain_sum = jnp.zeros((1, 8, WIDE), f32)
    forward_outs, backward_outs = [], []
    kept = []
    for tick in range(ticks):
        first, final = tick == 0, tick + 1 == ticks
        send, keep, normed_back, hidden_back, grad_pre, gain_sum = local(
            functools.partial(tick_body, first),
            [
                out(bf16, 2, HALF, WIDE), out(f32, 2, HALF, WIDE), out(bf16, *whole),
                out(bf16, *whole), out(bf16, *whole), out(f32, 1, 8, WIDE),
            ],
            flags, near, far, s_near, s_far, norm_scaling, weight_in, weight_out, gain_sum,
            scalars=1, limit=28, flops=10 * HALF * 2 * WIDE * WIDE,
            scratch=[pltpu.VMEM((4 * HALF, WIDE), bf16), pltpu.VMEM(whole, bf16)],
        )
        kept.append((normed_back, grad_pre, hidden_back, near[1], far[1]))
        arrived = route(send, 0, 0, 1)
        if final:
            gain_in = route(gain_sum.astype(bf16), 0, 0, 1)
            last = (2 * Z + 1, OWN, WIDE)
            total, gain_sum, *blocks = local(
                last_split_body,
                [out(f32, *block), out(f32, 1, 8, WIDE)] + [out(bf16, *last)] * (Y - 1),
                keep, arrived, gain_sum, gain_in,
            )
            got = [route(b, 0, j + 1, 0) for j, b in enumerate(blocks)]
            own, *blocks = local(
                last_sum_body,
                [out(f32, 3, OWN, WIDE)] + [out(bf16, 3, OWN, WIDE)] * (Z - 1),
                total, gain_sum, *got,
            )
            got = [route(b, k + 1, 0, 0) for k, b in enumerate(blocks)]
            y_now, grad_x, gain_total = local(
                last_body,
                [out(bf16, OWN, WIDE), out(bf16, OWN, WIDE), out(f32, 1, WIDE)],
                flags, own, *got, near, s_near, norm_scaling, scalars=1,
            )
            forward_outs.append(y_now)
            backward_outs.append(grad_x)
            break
        passed = [later] if first else []
        total, *blocks = local(
            functools.partial(split_body, len(passed)),
            [out(f32, *block)] + [out(bf16, *block)] * (Y - 1) + [out(p.dtype, *p.shape) for p in passed],
            keep, arrived, *passed,
        )
        got = [route(b, 0, j + 1, 0) for j, b in enumerate(blocks[: Y - 1])]
        if first:
            later = blocks[-1]
            passed = [later] + [route(later, -k, 0, 0) for k in range(1, Z)]
        total, narrow, *rest = local(
            functools.partial(sum_body, len(passed)),
            [out(f32, *block), out(bf16, *block)] + [out(bf16, *block)] * (2 if first else 0),
            total, *got, *passed,
        )
        got = [route(narrow, k, 0, 0) for k in range(1, Z)]
        if first:
            later, entering = rest
            passed = [later] + [route(later, 0, -j, 0) for j in range(1, Y)]
        y_now, grad_x, *rest = local(
            functools.partial(finish_body, first, len(passed)),
            [out(bf16, NEAR, WIDE)] * 2 + [out(bf16, 2, HALF, WIDE)] * (1 if first else 0),
            flags, total, *got, near, s_near, norm_scaling, *passed, scalars=1,
        )
        forward_outs.append(y_now[:OWN])
        backward_outs.append(grad_x[:OWN])
        y_in, g_in = shifted(y_now, 1), shifted(grad_x, -1)
        if first:
            later_near = rest[0]
            later_far = route(later_near, 0, 0, 1)
        (rows,) = local(
            select_body, [out(bf16, *block)], flags, y_in, g_in, entering[tick], scalars=1
        )
        near = gather_y(rows)
        far = route(near, 0, 0, 1)
        s_near, s_far = later_near[tick], later_far[tick]

    normed_seq, grad_pre_seq, hidden_seq = (
        jnp.concatenate([k[i] for k in kept], axis=0) for i in range(3)
    )
    slope_seq = jnp.concatenate([rows for k in kept for rows in k[3:]], axis=0)
    grad_in = dot(normed_seq, grad_pre_seq, 0, 0).astype(bf16)
    grad_out = dot(hidden_seq, slope_seq, 0, 0).astype(bf16)
    return (
        jnp.stack(forward_outs)[None],
        jnp.stack(backward_outs)[None],
        grad_in[None],
        grad_out[None],
        gain_total,
    )


def solution(mesh):
    placed = (
        P(None, "dp", None),
        P("section", "dp", None),
        P("section", None, "dp", None),
        P("section", "dp", None),
        P(None, "dp", None),
        P("section", None),
        P("section", None, "dp"),
        P("section", "dp", None),
    )
    return jax.shard_map(
        on_device,
        mesh=mesh,
        in_specs=placed,
        out_specs=(
            P("section", None, "dp", None),
            P("section", None, "dp", None),
            P("section", None, "dp"),
            P("section", "dp", None),
            P("section", None),
        ),
        check_vma=False,
    )
```

```python
import functools

import jax
import jax.numpy as jnp
from jax import lax
from jax.experimental import pallas as pl
from jax.experimental.pallas import tpu as pltpu
from jax.sharding import PartitionSpec as P

gelu_coef = 0.7978845608028654
gelu_cubic = 0.044715
norm_eps = 1e-06
bf16 = jnp.bfloat16
f32 = jnp.float32

Z, Y, CORES = 4, 4, 2
ORDER = (0, 1, 3, 2)
OWN = 8
NEAR = OWN * Z
HALF = NEAR * Y
WIDE = 1024
CHUNKS = [slice(i, i + 256) for i in range(0, WIDE, 256)]
MIB = 1024 * 1024


def place(index):
    return index // (Y * CORES), index // CORES % Y, index % CORES


def route(value, xz, dy, dc):
    pairs = []
    for i in range(Z * Y * CORES):
        z, y, c = place(i)
        pairs.append((i, ((z ^ xz) * Y + (y + dy) % Y) * CORES + (c ^ dc)))
    return lax.ppermute(value, "dp", pairs)


def shifted(value, by):
    devices = lax.axis_size("section")
    return lax.ppermute(value, "section", [(i, (i + by) % devices) for i in range(devices)])


def out(dtype, *shape):
    return jax.ShapeDtypeStruct(shape, dtype)


def local(body, outs, *operands, scalars=0, loose=0, limit=8, scratch=(), flops=0):
    size = sum(math_size(o) for o in operands) + sum(math_size(o) for o in outs)
    specs = [pl.BlockSpec(memory_space=pltpu.SMEM)] * scalars
    specs += [pl.BlockSpec(memory_space=pltpu.VMEM)] * (len(operands) - scalars - loose)
    specs += [pl.BlockSpec(memory_space=pl.ANY)] * loose
    return pl.pallas_call(
        body,
        out_shape=tuple(outs),
        in_specs=specs,
        out_specs=tuple([pl.BlockSpec(memory_space=pltpu.VMEM)] * len(outs)),
        scratch_shapes=list(scratch),
        compiler_params=pltpu.CompilerParams(vmem_limit_bytes=limit * MIB),
        cost_estimate=pl.CostEstimate(flops=flops, bytes_accessed=size, transcendentals=0),
    )(*operands)


def math_size(array):
    total = jnp.dtype(array.dtype).itemsize
    for d in array.shape:
        total *= d
    return total


def dot(a, b, ca, cb):
    return lax.dot_general(a, b, (((ca,), (cb,)), ((), ())), preferred_element_type=f32)


def rms_factor(wide):
    return lax.rsqrt(jnp.mean(wide * wide, axis=-1, keepdims=True) + norm_eps)


def gelu_parts(pre):
    square = pre * pre
    tangent = jnp.tanh(pre * (gelu_coef + (gelu_coef * gelu_cubic) * square))
    gate = 0.5 + 0.5 * tangent
    value = pre * gate
    slope = gate + value * (1.0 - tangent) * (gelu_coef + (3.0 * gelu_coef * gelu_cubic) * square)
    return value, slope


def begin_body(
    flags, near, far, gain, w_in, w_out, gain_was,
    send, normed_back, hidden_near, hidden_back, grad_pre, gain_sum,
    normed, hidden_far,
):
    is_last = flags[1] == 1
    row = gain[...]
    for i, half in enumerate((near, far)):
        x = half[0].astype(f32)
        normed[i * HALF : (i + 1) * HALF] = (x * rms_factor(x) * row).astype(bf16)
        x = jnp.where(is_last, x, half[2].astype(f32))
        value = (x * rms_factor(x) * row).astype(bf16)
        normed[(2 + i) * HALF : (3 + i) * HALF] = value
        normed_back[i * HALF : (i + 1) * HALF] = value

    for cols in CHUNKS:
        pre = dot(normed[...], w_in[:, cols], 1, 0)
        value, _ = gelu_parts(pre[: 2 * HALF])
        hidden_near[:, cols] = value[:HALF].astype(bf16)
        hidden_far[:, cols] = value[HALF:].astype(bf16)
        value, slope = gelu_parts(pre[2 * HALF :])
        hidden_back[:, cols] = value.astype(bf16)
        for i, half in enumerate((near, far)):
            rows = slice(i * HALF, (i + 1) * HALF)
            grad_pre[rows, cols] = (dot(half[1], w_out[cols, :], 1, 1) * slope[rows]).astype(bf16)

    for cols in CHUNKS:
        send[0, :, cols] = dot(hidden_far[...], w_out[:, cols], 1, 0).astype(bf16)
        part = dot(grad_pre[HALF:, :], w_in[cols, :], 1, 1)
        send[1, :, cols] = part.astype(bf16)
        gain_sum[0, :, cols] = gain_was[0, :, cols] + gain_term(part, normed_back[HALF:, cols])


def gain_term(part, normed):
    return jnp.sum((part * normed.astype(f32)).reshape(-1, 8, part.shape[-1]), axis=0)


def end_body(hidden_near, grad_pre, normed_back, w_in, w_out, gain_was, keep, gain_sum):
    for cols in CHUNKS:
        keep[0, :, cols] = dot(hidden_near[...], w_out[:, cols], 1, 0)
        part = dot(grad_pre[:HALF, :], w_in[cols, :], 1, 1)
        keep[1, :, cols] = part
        gain_sum[0, :, cols] = gain_was[0, :, cols] + gain_term(part, normed_back[:HALF, cols])


def split_body(keep, arrived, total, *blocks):
    for j in range(Y):
        rows = slice(j * NEAR, (j + 1) * NEAR)
        value = keep[:, rows] + arrived[:, rows].astype(f32)
        if j == 0:
            total[...] = value
        else:
            blocks[j - 1][...] = value.astype(bf16)


def stack_z(parts):
    return jnp.concatenate([p.astype(f32) for p in parts], axis=-2).astype(bf16)


def sum_body(passed, total, *refs):
    value = total[...]
    for r in refs[: Y - 1]:
        value = value + r[...].astype(f32)
    given, outs = refs[Y - 1 : Y - 1 + passed], refs[Y - 1 + passed :]
    outs[0][...] = value
    outs[1][...] = value[0].astype(bf16)
    outs[2][...] = value[1].astype(bf16)
    if passed:
        value = stack_z([r[...] for r in given])
        for i, ref in enumerate(outs[3:]):
            ref[...] = value[i]


def swap_one(rows):
    rows = [rows[i * OWN : (i + 1) * OWN] for i in range(Z)]
    return jnp.concatenate([rows[1], rows[0], rows[3], rows[2]], axis=0)


def swap_three(rows):
    return jnp.concatenate([rows[2 * OWN :], rows[: 2 * OWN]], axis=0)


def middle_body(total, fwd_in, bwd_in, ahead, summed, fwd_out, bwd_out, ahead_out):
    fwd = total[0] + swap_one(fwd_in[...].astype(f32))
    bwd = total[1] + swap_three(bwd_in[...].astype(f32))
    summed[0] = fwd
    summed[1] = bwd
    fwd_out[...] = fwd.astype(bf16)
    bwd_out[...] = bwd.astype(bf16)
    ahead_out[...] = ahead[...]


def norm_backward(x, grad_normed, grad_rows, row):
    factor = rms_factor(x)
    weighted = row * grad_normed
    inner = jnp.mean(weighted * x, axis=-1, keepdims=True)
    return grad_rows + factor * weighted - x * (factor * factor * factor) * inner


def finish_body(flags, total, fwd_in, bwd_in, near, gain, y_now, grad_x):
    fwd = total[0] + swap_three(fwd_in[...].astype(f32))
    bwd = total[1] + swap_one(bwd_in[...].astype(f32))
    x = near[0, :NEAR].astype(f32)
    y_now[...] = (x + fwd).astype(bf16)
    x_back = jnp.where(flags[1] == 1, x, near[2, :NEAR].astype(f32))
    grads = near[1, :NEAR].astype(f32)
    grad_x[...] = norm_backward(x_back, bwd, grads, gain[...]).astype(bf16)


def join_body(*refs):
    for j, part in enumerate(refs[:Y]):
        refs[-1][:, j * NEAR : (j + 1) * NEAR, :] = part[...]


def join_z_body(one, two, *refs):
    refs[-1][...] = stack_z([one[...], two[...]])


def hold_body(value, _, same):
    same[...] = value[...]


def select_body(flags, y_in, g_in, entering, *refs):
    rows = refs[-1]
    own = entering[...].astype(f32)
    rows[0] = jnp.where(flags[0] == 1, own, y_in[...].astype(f32)).astype(bf16)
    rows[1] = jnp.where(flags[1] == 1, own, g_in[...].astype(f32)).astype(bf16)


def enter_body(*refs):
    for j in range(Y):
        block = slice(j * NEAR, (j + 1) * NEAR)
        refs[-1][:2, block] = refs[j][...]
        refs[-1][2, block] = refs[Y + j][...]


def hold(value, until):
    return local(hold_body, [out(value.dtype, *value.shape)], value, until)[0]


def gather_y(rows):
    return [rows] + [route(rows, 0, -j, 0) for j in range(1, Y)]


def last_split_body(keep, arrived, gain_sum, gain_in, total, gain_total, *blocks):
    gain_value = gain_sum[...] + gain_in[...].astype(f32)
    gain_total[...] = gain_value
    for j in range(Y):
        rows = slice(j * NEAR, (j + 1) * NEAR)
        value = keep[:, rows] + arrived[:, rows].astype(f32)
        if j == 0:
            total[...] = value
        else:
            for i in range(2):
                for k in range(Z):
                    blocks[j - 1][i * Z + k] = value[i, k * OWN : (k + 1) * OWN].astype(bf16)
            blocks[j - 1][2 * Z] = gain_value[0].astype(bf16)


def last_sum_body(total, gain_total, r1, r2, r3, _, own, block):
    gain_value = gain_total[0]
    for ref in (r1, r2, r3):
        gain_value = gain_value + ref[2 * Z].astype(f32)
    for k in range(Z):
        for i in range(2):
            value = total[i, k * OWN : (k + 1) * OWN]
            for ref in (r1, r2, r3):
                value = value + ref[i * Z + k].astype(f32)
            if k < 2:
                own[2 * k + i] = value
            else:
                block[2 * (k - 2) + i] = value.astype(bf16)
    own[4] = gain_value
    block[4] = gain_value.astype(bf16)


def last_middle_body(own, got, _, summed, block):
    for i in range(2):
        summed[i] = own[i] + got[i].astype(f32)
        block[i] = (own[2 + i] + got[2 + i].astype(f32)).astype(bf16)
    value = own[4] + got[4].astype(f32)
    summed[2] = value
    block[2] = value.astype(bf16)


def last_body(flags, own, got, near, gain, *refs):
    before, (y_all, grad_all, gain_total) = refs[:-3], refs[-3:]
    for t in range(len(before) // 2):
        y_all[t] = before[2 * t][:16].astype(f32)[:OWN].astype(bf16)
        grad_all[t] = before[2 * t + 1][:16].astype(f32)[:OWN].astype(bf16)
    fwd, bwd, gain_value = (own[i] + got[i].astype(f32) for i in range(3))
    x = near[0, :16].astype(f32)[:OWN]
    y_all[len(before) // 2] = (x + fwd).astype(bf16)
    x_back = jnp.where(flags[1] == 1, x, near[2, :16].astype(f32)[:OWN])
    grads = near[1, :16].astype(f32)[:OWN]
    grad_all[len(before) // 2] = norm_backward(x_back, bwd, grads, gain[...]).astype(bf16)
    gain_total[...] = jnp.sum(gain_value, axis=0, keepdims=True) / gain[...]


def on_device(
    novel_batch_seq,
    transit_activity,
    saved_prior_entries,
    waiting_loss_slope,
    loss_slope_seq,
    norm_scaling,
    entering_matrix,
    leaving_matrix,
):
    section_pos = lax.axis_index("section")
    section_count = lax.axis_size("section")
    ticks = novel_batch_seq.shape[0]
    depth = saved_prior_entries.shape[1]
    weight_in = entering_matrix[0]
    weight_out = leaving_matrix[0]
    is_first = section_pos == 0
    is_last = section_pos == section_count - 1
    flags = jnp.stack([is_first, is_last]).astype(jnp.int32)
    x_first = jnp.where(is_first, novel_batch_seq[0], transit_activity[0])
    g_first = jnp.where(is_last, loss_slope_seq[0], waiting_loss_slope[0])
    stored = []
    for tick in range(ticks):
        index = tick + 2 * section_pos
        held = lax.dynamic_index_in_dim(
            saved_prior_entries[0], jnp.minimum(index, depth - 1), 0, keepdims=False
        )
        stored.append(jnp.where(index < depth, held, x_first))
    entering = [jnp.where(is_last, loss_slope_seq[t], novel_batch_seq[t]) for t in range(1, ticks)]
    begin = jnp.stack([x_first, g_first, stored[0]])
    later = jnp.stack(stored[1:] + entering)

    (rows,) = local(join_z_body, [out(bf16, 3, 2 * OWN, WIDE)], begin, route(begin, 1, 0, 0))
    (rows,) = local(join_z_body, [out(bf16, 3, NEAR, WIDE)], rows, route(rows, 3, 0, 0))
    parts = gather_y(rows)
    later = hold(later, parts[1])
    beside = route(later, 1, 0, 0)
    (near,) = local(join_body, [out(bf16, 3, HALF, WIDE)], *parts, beside)
    (later,) = local(join_z_body, [out(bf16, 4, 2 * OWN, WIDE)], later, beside)
    passed = [later, route(later, 3, 0, 0)]

    block = (2, NEAR, WIDE)
    whole = (2 * HALF, WIDE)
    flops = 2 * HALF * WIDE * WIDE
    gain_sum = jnp.zeros((1, 8, WIDE), f32)
    ended, kept = [], []
    for tick in range(ticks):
        first, final = tick == 0, tick + 1 == ticks
        far = route(near, 0, 0, 1)
        send, normed_back, hidden_near, hidden_back, grad_pre, gain_sum = local(
            begin_body,
            [
                out(bf16, 2, HALF, WIDE), out(bf16, *whole), out(bf16, HALF, WIDE),
                out(bf16, *whole), out(bf16, *whole), out(f32, 1, 8, WIDE),
            ],
            flags, near, far, norm_scaling, weight_in, weight_out, gain_sum,
            scalars=1, limit=24, flops=8 * flops,
            scratch=[pltpu.VMEM((4 * HALF, WIDE), bf16), pltpu.VMEM((HALF, WIDE), bf16)],
        )
        kept.append((normed_back, grad_pre, hidden_back, near[1], far[1]))
        arrived = route(send, 0, 0, 1)
        keep, gain_sum = local(
            end_body, [out(f32, 2, HALF, WIDE), out(f32, 1, 8, WIDE)],
            hidden_near, grad_pre, normed_back, weight_in, weight_out, gain_sum,
            limit=24, flops=2 * flops,
        )
        if final:
            gain_in = route(gain_sum.astype(bf16), 0, 0, 1)
            last = (2 * Z + 1, OWN, WIDE)
            total, gain_sum, *blocks = local(
                last_split_body,
                [out(f32, *block), out(f32, 1, 8, WIDE)] + [out(bf16, *last)] * (Y - 1),
                keep, arrived, gain_sum, gain_in,
            )
            got = [route(b, 0, j + 1, 0) for j, b in enumerate(blocks)]
            kept[-1] = kept[-1][:4] + (hold(far[1], got[0]),)
            hidden_seq = jnp.concatenate([k[2] for k in kept], axis=0)
            slope_seq = jnp.concatenate([rows for k in kept for rows in k[3:]], axis=0)
            grad_out = dot(hidden_seq, slope_seq, 0, 0).astype(bf16)
            own, block = local(
                last_sum_body, [out(f32, 5, OWN, WIDE), out(bf16, 5, OWN, WIDE)],
                total, gain_sum, *got, grad_out, loose=1,
            )
            normed_seq, grad_pre_seq = (
                jnp.concatenate([k[i] for k in kept], axis=0) for i in range(2)
            )
            grad_in = dot(normed_seq, grad_pre_seq, 0, 0).astype(bf16)
            own, block = local(
                last_middle_body, [out(f32, 3, OWN, WIDE), out(bf16, 3, OWN, WIDE)],
                own, route(block, 3, 0, 0), grad_in, loose=1,
            )
            got = route(block, 1, 0, 0)
            forward_out, backward_out, gain_total = local(
                last_body,
                [out(bf16, ticks, OWN, WIDE), out(bf16, ticks, OWN, WIDE), out(f32, 1, WIDE)],
                flags, own, got, near, norm_scaling, *ended, scalars=1,
            )
            break
        total, *blocks = local(
            split_body, [out(f32, *block)] + [out(bf16, *block)] * (Y - 1), keep, arrived
        )
        got = [route(b, 0, j + 1, 0) for j, b in enumerate(blocks)]
        total, fwd, bwd, *rest = local(
            functools.partial(sum_body, len(passed)),
            [out(f32, *block)] + [out(bf16, NEAR, WIDE)] * (6 if first else 2),
            total, *got, *passed,
        )
        if first:
            ahead, entering, passed = rest[:2], rest[2:], []
        total, fwd, bwd, beside = local(
            middle_body,
            [out(f32, *block)] + [out(bf16, NEAR, WIDE)] * 3,
            total, route(fwd, 1, 0, 0), route(bwd, 3, 0, 0), ahead[tick],
        )
        beside = gather_y(beside)
        y_now, grad_x = local(
            finish_body, [out(bf16, NEAR, WIDE)] * 2,
            flags, total, route(fwd, 3, 0, 0), route(bwd, 1, 0, 0), near, norm_scaling, scalars=1,
        )
        ended += [y_now, grad_x]
        y_in, g_in = shifted(y_now, 1), shifted(grad_x, -1)
        (rows,) = local(
            select_body, [out(bf16, *block)], flags, y_in, g_in, entering[tick], *beside,
            scalars=1,
        )
        (near,) = local(enter_body, [out(bf16, 3, HALF, WIDE)], *gather_y(rows), *beside)

    return (
        forward_out[None],
        backward_out[None],
        grad_in[None],
        grad_out[None],
        gain_total,
    )


def solution(mesh):
    placed = (
        P(None, "dp", None),
        P("section", "dp", None),
        P("section", None, "dp", None),
        P("section", "dp", None),
        P(None, "dp", None),
        P("section", None),
        P("section", None, "dp"),
        P("section", "dp", None),
    )
    return jax.shard_map(
        on_device,
        mesh=mesh,
        in_specs=placed,
        out_specs=(
            P("section", None, "dp", None),
            P("section", None, "dp", None),
            P("section", None, "dp"),
            P("section", "dp", None),
            P("section", None),
        ),
        check_vma=False,
    )
```

```python
import functools

import jax
import jax.numpy as jnp
from jax import lax
from jax.experimental import pallas as pl
from jax.experimental.pallas import tpu as pltpu
from jax.sharding import PartitionSpec as P

gelu_coef = 0.7978845608028654
gelu_cubic = 0.044715
norm_eps = 1e-06
bf16 = jnp.bfloat16
f32 = jnp.float32

Z, Y, CORES = 4, 4, 2
ORDER = (0, 1, 3, 2)
OWN = 8
NEAR = OWN * Z
HALF = NEAR * Y
WIDE = 1024
CHUNKS = [slice(i, i + 256) for i in range(0, WIDE, 256)]
MIB = 1024 * 1024


def place(index):
    return index // (Y * CORES), index // CORES % Y, index % CORES


def route(value, xz, dy, dc):
    pairs = []
    for i in range(Z * Y * CORES):
        z, y, c = place(i)
        pairs.append((i, ((z ^ xz) * Y + (y + dy) % Y) * CORES + (c ^ dc)))
    return lax.ppermute(value, "dp", pairs)


def shifted(value, by):
    devices = lax.axis_size("section")
    return lax.ppermute(value, "section", [(i, (i + by) % devices) for i in range(devices)])


def out(dtype, *shape):
    return jax.ShapeDtypeStruct(shape, dtype)


def local(body, outs, *operands, scalars=0, loose=0, limit=8, scratch=(), flops=0):
    size = sum(math_size(o) for o in operands) + sum(math_size(o) for o in outs)
    specs = [pl.BlockSpec(memory_space=pltpu.SMEM)] * scalars
    specs += [pl.BlockSpec(memory_space=pltpu.VMEM)] * (len(operands) - scalars - loose)
    specs += [pl.BlockSpec(memory_space=pl.ANY)] * loose
    return pl.pallas_call(
        body,
        out_shape=tuple(outs),
        in_specs=specs,
        out_specs=tuple([pl.BlockSpec(memory_space=pltpu.VMEM)] * len(outs)),
        scratch_shapes=list(scratch),
        compiler_params=pltpu.CompilerParams(vmem_limit_bytes=limit * MIB),
        cost_estimate=pl.CostEstimate(flops=flops, bytes_accessed=size, transcendentals=0),
    )(*operands)


def math_size(array):
    total = jnp.dtype(array.dtype).itemsize
    for d in array.shape:
        total *= d
    return total


def dot(a, b, ca, cb):
    return lax.dot_general(a, b, (((ca,), (cb,)), ((), ())), preferred_element_type=f32)


def rms_factor(wide):
    return lax.rsqrt(jnp.mean(wide * wide, axis=-1, keepdims=True) + norm_eps)


def gelu_parts(pre):
    square = pre * pre
    tangent = jnp.tanh(pre * (gelu_coef + (gelu_coef * gelu_cubic) * square))
    gate = 0.5 + 0.5 * tangent
    value = pre * gate
    slope = gate + value * (1.0 - tangent) * (gelu_coef + (3.0 * gelu_coef * gelu_cubic) * square)
    return value, slope


def first_half(flags, rows, gain, w_in, w_out, normed_back, hidden, hidden_back, grad_pre, normed):
    row = gain[...]
    x = rows[0].astype(f32)
    normed[:HALF] = (x * rms_factor(x) * row).astype(bf16)
    x = jnp.where(flags[1] == 1, x, rows[2].astype(f32))
    value = (x * rms_factor(x) * row).astype(bf16)
    normed[HALF:] = value
    normed_back[...] = value
    for cols in CHUNKS:
        pre = dot(normed[...], w_in[:, cols], 1, 0)
        value, _ = gelu_parts(pre[:HALF])
        hidden[:, cols] = value.astype(bf16)
        value, slope = gelu_parts(pre[HALF:])
        hidden_back[:, cols] = value.astype(bf16)
        grad_pre[:, cols] = (dot(rows[1], w_out[cols, :], 1, 1) * slope).astype(bf16)


def near_body(flags, near, gain, w_in, w_out, *refs):
    first_half(flags, near, gain, w_in, w_out, *refs)


def far_body(
    flags, far, gain, w_in, w_out, gain_was, _,
    normed_back, hidden_back, grad_pre, send, gain_sum, hidden, normed,
):
    first_half(flags, far, gain, w_in, w_out, normed_back, hidden, hidden_back, grad_pre, normed)
    for cols in CHUNKS:
        send[0, :, cols] = dot(hidden[...], w_out[:, cols], 1, 0).astype(bf16)
        part = dot(grad_pre[...], w_in[cols, :], 1, 1)
        send[1, :, cols] = part.astype(bf16)
        gain_sum[0, :, cols] = gain_was[0, :, cols] + gain_term(part, normed_back[:, cols])


def gain_term(part, normed):
    return jnp.sum((part * normed.astype(f32)).reshape(-1, 8, part.shape[-1]), axis=0)


def end_body(hidden_near, grad_pre, normed_back, w_in, w_out, gain_was, keep, gain_sum):
    for cols in CHUNKS:
        keep[0, :, cols] = dot(hidden_near[...], w_out[:, cols], 1, 0)
        part = dot(grad_pre[...], w_in[cols, :], 1, 1)
        keep[1, :, cols] = part
        gain_sum[0, :, cols] = gain_was[0, :, cols] + gain_term(part, normed_back[:, cols])


def split_body(keep, arrived, total, *blocks):
    for j in range(Y):
        rows = slice(j * NEAR, (j + 1) * NEAR)
        value = keep[:, rows] + arrived[:, rows].astype(f32)
        if j == 0:
            total[...] = value
        else:
            blocks[j - 1][...] = value.astype(bf16)


def stack_z(parts):
    return jnp.concatenate([p.astype(f32) for p in parts], axis=-2).astype(bf16)


def sum_body(passed, total, *refs):
    value = total[...]
    for r in refs[: Y - 1]:
        value = value + r[...].astype(f32)
    given, outs = refs[Y - 1 : Y - 1 + passed], refs[Y - 1 + passed :]
    outs[0][...] = value
    outs[1][...] = value[0].astype(bf16)
    outs[2][...] = value[1].astype(bf16)
    if passed:
        value = stack_z([r[...] for r in given])
        for i, ref in enumerate(outs[3:]):
            ref[...] = value[i]


def swap_one(rows):
    rows = [rows[i * OWN : (i + 1) * OWN] for i in range(Z)]
    return jnp.concatenate([rows[1], rows[0], rows[3], rows[2]], axis=0)


def swap_three(rows):
    return jnp.concatenate([rows[2 * OWN :], rows[: 2 * OWN]], axis=0)


def middle_body(total, fwd_in, bwd_in, ahead, summed, fwd_out, bwd_out, ahead_out):
    fwd = total[0] + swap_one(fwd_in[...].astype(f32))
    bwd = total[1] + swap_three(bwd_in[...].astype(f32))
    summed[0] = fwd
    summed[1] = bwd
    fwd_out[...] = fwd.astype(bf16)
    bwd_out[...] = bwd.astype(bf16)
    ahead_out[...] = ahead[...]


def norm_backward(x, grad_normed, grad_rows, row):
    factor = rms_factor(x)
    weighted = row * grad_normed
    inner = jnp.mean(weighted * x, axis=-1, keepdims=True)
    return grad_rows + factor * weighted - x * (factor * factor * factor) * inner


def finish_body(flags, total, fwd_in, bwd_in, near, gain, y_now, grad_x):
    fwd = total[0] + swap_three(fwd_in[...].astype(f32))
    bwd = total[1] + swap_one(bwd_in[...].astype(f32))
    x = near[0, :NEAR].astype(f32)
    y_now[...] = (x + fwd).astype(bf16)
    x_back = jnp.where(flags[1] == 1, x, near[2, :NEAR].astype(f32))
    grads = near[1, :NEAR].astype(f32)
    grad_x[...] = norm_backward(x_back, bwd, grads, gain[...]).astype(bf16)


def join_body(*refs):
    for j, part in enumerate(refs[:Y]):
        refs[-1][:, j * NEAR : (j + 1) * NEAR, :] = part[...]


def join_z_body(one, two, *refs):
    refs[-1][...] = stack_z([one[...], two[...]])


def hold_body(value, _, same):
    same[...] = value[...]


def select_body(flags, y_in, g_in, entering, *refs):
    rows = refs[-1]
    own = entering[...].astype(f32)
    rows[0] = jnp.where(flags[0] == 1, own, y_in[...].astype(f32)).astype(bf16)
    rows[1] = jnp.where(flags[1] == 1, own, g_in[...].astype(f32)).astype(bf16)


def enter_body(*refs):
    for j in range(Y):
        block = slice(j * NEAR, (j + 1) * NEAR)
        refs[-1][:2, block] = refs[j][...]
        refs[-1][2, block] = refs[Y + j][...]


def hold(value, until):
    return local(hold_body, [out(value.dtype, *value.shape)], value, until)[0]


def gather_y(rows):
    return [rows] + [route(rows, 0, -j, 0) for j in range(1, Y)]


def last_split_body(keep, arrived, gain_sum, gain_in, total, gain_total, *blocks):
    gain_value = gain_sum[...] + gain_in[...].astype(f32)
    gain_total[...] = gain_value
    for j in range(Y):
        rows = slice(j * NEAR, (j + 1) * NEAR)
        value = keep[:, rows] + arrived[:, rows].astype(f32)
        if j == 0:
            total[...] = value
        else:
            for i in range(2):
                for k in range(Z):
                    blocks[j - 1][i * Z + k] = value[i, k * OWN : (k + 1) * OWN].astype(bf16)
            blocks[j - 1][2 * Z] = gain_value[0].astype(bf16)


def last_sum_body(total, gain_total, r1, r2, r3, _, own, block):
    gain_value = gain_total[0]
    for ref in (r1, r2, r3):
        gain_value = gain_value + ref[2 * Z].astype(f32)
    for k in range(Z):
        for i in range(2):
            value = total[i, k * OWN : (k + 1) * OWN]
            for ref in (r1, r2, r3):
                value = value + ref[i * Z + k].astype(f32)
            if k < 2:
                own[2 * k + i] = value
            else:
                block[2 * (k - 2) + i] = value.astype(bf16)
    own[4] = gain_value
    block[4] = gain_value.astype(bf16)


def last_middle_body(own, got, _, summed, block):
    for i in range(2):
        summed[i] = own[i] + got[i].astype(f32)
        block[i] = (own[2 + i] + got[2 + i].astype(f32)).astype(bf16)
    value = own[4] + got[4].astype(f32)
    summed[2] = value
    block[2] = value.astype(bf16)


def last_body(flags, own, got, near, gain, *refs):
    before, (y_all, grad_all, gain_total) = refs[:-3], refs[-3:]
    for t in range(len(before) // 2):
        y_all[t] = before[2 * t][:16].astype(f32)[:OWN].astype(bf16)
        grad_all[t] = before[2 * t + 1][:16].astype(f32)[:OWN].astype(bf16)
    fwd, bwd, gain_value = (own[i] + got[i].astype(f32) for i in range(3))
    x = near[0, :16].astype(f32)[:OWN]
    y_all[len(before) // 2] = (x + fwd).astype(bf16)
    x_back = jnp.where(flags[1] == 1, x, near[2, :16].astype(f32)[:OWN])
    grads = near[1, :16].astype(f32)[:OWN]
    grad_all[len(before) // 2] = norm_backward(x_back, bwd, grads, gain[...]).astype(bf16)
    gain_total[...] = jnp.sum(gain_value, axis=0, keepdims=True) / gain[...]


def on_device(
    novel_batch_seq,
    transit_activity,
    saved_prior_entries,
    waiting_loss_slope,
    loss_slope_seq,
    norm_scaling,
    entering_matrix,
    leaving_matrix,
):
    section_pos = lax.axis_index("section")
    section_count = lax.axis_size("section")
    ticks = novel_batch_seq.shape[0]
    depth = saved_prior_entries.shape[1]
    weight_in = entering_matrix[0]
    weight_out = leaving_matrix[0]
    is_first = section_pos == 0
    is_last = section_pos == section_count - 1
    flags = jnp.stack([is_first, is_last]).astype(jnp.int32)
    x_first = jnp.where(is_first, novel_batch_seq[0], transit_activity[0])
    g_first = jnp.where(is_last, loss_slope_seq[0], waiting_loss_slope[0])
    stored = []
    for tick in range(ticks):
        index = tick + 2 * section_pos
        held = lax.dynamic_index_in_dim(
            saved_prior_entries[0], jnp.minimum(index, depth - 1), 0, keepdims=False
        )
        stored.append(jnp.where(index < depth, held, x_first))
    entering = [jnp.where(is_last, loss_slope_seq[t], novel_batch_seq[t]) for t in range(1, ticks)]
    begin = jnp.stack([x_first, g_first, stored[0]])
    later = jnp.stack(stored[1:] + entering)

    (rows,) = local(join_z_body, [out(bf16, 3, 2 * OWN, WIDE)], begin, route(begin, 1, 0, 0))
    (rows,) = local(join_z_body, [out(bf16, 3, NEAR, WIDE)], rows, route(rows, 3, 0, 0))
    parts = gather_y(rows)
    later = hold(later, parts[1])
    beside = route(later, 1, 0, 0)
    (near,) = local(join_body, [out(bf16, 3, HALF, WIDE)], *parts, beside)
    (later,) = local(join_z_body, [out(bf16, 4, 2 * OWN, WIDE)], later, beside)
    passed = [later, route(later, 3, 0, 0)]

    block = (2, NEAR, WIDE)
    whole, half = (2 * HALF, WIDE), (HALF, WIDE)
    flops = 2 * HALF * WIDE * WIDE
    gain_sum = jnp.zeros((1, 8, WIDE), f32)
    ended, kept = [], []
    for tick in range(ticks):
        first, final = tick == 0, tick + 1 == ticks
        far = route(near, 0, 0, 1)
        back_near, hidden_near, hidden_back_near, pre_near = local(
            near_body, [out(bf16, *half)] * 4,
            flags, near, norm_scaling, weight_in, weight_out,
            scalars=1, limit=24, flops=3 * flops, scratch=[pltpu.VMEM(whole, bf16)],
        )
        back_far, hidden_back_far, pre_far, send, gain_sum = local(
            far_body, [out(bf16, *half)] * 3 + [out(bf16, 2, HALF, WIDE), out(f32, 1, 8, WIDE)],
            flags, far, norm_scaling, weight_in, weight_out, gain_sum, hidden_near,
            scalars=1, limit=24, flops=5 * flops,
            scratch=[pltpu.VMEM(half, bf16), pltpu.VMEM(whole, bf16)],
        )
        kept.append(
            [(back_near, back_far), (pre_near, pre_far), (hidden_back_near, hidden_back_far), (near[1], far[1])]
        )
        arrived = route(send, 0, 0, 1)
        keep, gain_sum = local(
            end_body, [out(f32, 2, HALF, WIDE), out(f32, 1, 8, WIDE)],
            hidden_near, pre_near, back_near, weight_in, weight_out, gain_sum,
            limit=24, flops=2 * flops,
        )
        if final:
            gain_in = route(gain_sum.astype(bf16), 0, 0, 1)
            last = (2 * Z + 1, OWN, WIDE)
            total, gain_sum, *blocks = local(
                last_split_body,
                [out(f32, *block), out(f32, 1, 8, WIDE)] + [out(bf16, *last)] * (Y - 1),
                keep, arrived, gain_sum, gain_in,
            )
            got = [route(b, 0, j + 1, 0) for j, b in enumerate(blocks)]
            kept[-1][3] = (near[1], hold(far[1], got[0]))
            normed_seq, grad_pre_seq, hidden_seq, slope_seq = (
                jnp.concatenate([rows for k in kept for rows in k[i]], axis=0) for i in range(4)
            )
            grad_out = dot(hidden_seq, slope_seq, 0, 0).astype(bf16)
            own, block = local(
                last_sum_body, [out(f32, 5, OWN, WIDE), out(bf16, 5, OWN, WIDE)],
                total, gain_sum, *got, grad_out, loose=1,
            )
            grad_in = dot(normed_seq, grad_pre_seq, 0, 0).astype(bf16)
            own, block = local(
                last_middle_body, [out(f32, 3, OWN, WIDE), out(bf16, 3, OWN, WIDE)],
                own, route(block, 3, 0, 0), grad_in, loose=1,
            )
            got = route(block, 1, 0, 0)
            forward_out, backward_out, gain_total = local(
                last_body,
                [out(bf16, ticks, OWN, WIDE), out(bf16, ticks, OWN, WIDE), out(f32, 1, WIDE)],
                flags, own, got, near, norm_scaling, *ended, scalars=1,
            )
            break
        total, *blocks = local(
            split_body, [out(f32, *block)] + [out(bf16, *block)] * (Y - 1), keep, arrived
        )
        got = [route(b, 0, j + 1, 0) for j, b in enumerate(blocks)]
        total, fwd, bwd, *rest = local(
            functools.partial(sum_body, len(passed)),
            [out(f32, *block)] + [out(bf16, NEAR, WIDE)] * (6 if first else 2),
            total, *got, *passed,
        )
        if first:
            ahead, entering, passed = rest[:2], rest[2:], []
        total, fwd, bwd, beside = local(
            middle_body,
            [out(f32, *block)] + [out(bf16, NEAR, WIDE)] * 3,
            total, route(fwd, 1, 0, 0), route(bwd, 3, 0, 0), ahead[tick],
        )
        beside = gather_y(beside)
        y_now, grad_x = local(
            finish_body, [out(bf16, NEAR, WIDE)] * 2,
            flags, total, route(fwd, 3, 0, 0), route(bwd, 1, 0, 0), near, norm_scaling, scalars=1,
        )
        ended += [y_now, grad_x]
        y_in, g_in = shifted(y_now, 1), shifted(grad_x, -1)
        (rows,) = local(
            select_body, [out(bf16, *block)], flags, y_in, g_in, entering[tick], *beside,
            scalars=1,
        )
        (near,) = local(enter_body, [out(bf16, 3, HALF, WIDE)], *gather_y(rows), *beside)

    return (
        forward_out[None],
        backward_out[None],
        grad_in[None],
        grad_out[None],
        gain_total,
    )


def solution(mesh):
    placed = (
        P(None, "dp", None),
        P("section", "dp", None),
        P("section", None, "dp", None),
        P("section", "dp", None),
        P(None, "dp", None),
        P("section", None),
        P("section", None, "dp"),
        P("section", "dp", None),
    )
    return jax.shard_map(
        on_device,
        mesh=mesh,
        in_specs=placed,
        out_specs=(
            P("section", None, "dp", None),
            P("section", None, "dp", None),
            P("section", None, "dp"),
            P("section", "dp", None),
            P("section", None),
        ),
        check_vma=False,
    )
```

```python
import functools

import jax
import jax.numpy as jnp
from jax import lax
from jax.experimental import pallas as pl
from jax.experimental.pallas import tpu as pltpu
from jax.sharding import PartitionSpec as P

gelu_coef = 0.7978845608028654
gelu_cubic = 0.044715
norm_eps = 1e-06
bf16 = jnp.bfloat16
f32 = jnp.float32

Z, Y, CORES = 4, 4, 2
ORDER = (0, 1, 3, 2)
OWN = 8
NEAR = OWN * Z
HALF = NEAR * Y
WIDE = 1024
CHUNKS = [slice(i, i + 256) for i in range(0, WIDE, 256)]
MIB = 1024 * 1024


def place(index):
    return index // (Y * CORES), index // CORES % Y, index % CORES


def route(value, xz, dy, dc):
    pairs = []
    for i in range(Z * Y * CORES):
        z, y, c = place(i)
        pairs.append((i, ((z ^ xz) * Y + (y + dy) % Y) * CORES + (c ^ dc)))
    return lax.ppermute(value, "dp", pairs)


def shifted(value, by):
    devices = lax.axis_size("section")
    return lax.ppermute(value, "section", [(i, (i + by) % devices) for i in range(devices)])


def out(dtype, *shape):
    return jax.ShapeDtypeStruct(shape, dtype)


def local(body, outs, *operands, scalars=0, loose=0, limit=8, scratch=(), flops=0):
    size = sum(math_size(o) for o in operands) + sum(math_size(o) for o in outs)
    specs = [pl.BlockSpec(memory_space=pltpu.SMEM)] * scalars
    specs += [pl.BlockSpec(memory_space=pltpu.VMEM)] * (len(operands) - scalars - loose)
    specs += [pl.BlockSpec(memory_space=pl.ANY)] * loose
    return pl.pallas_call(
        body,
        out_shape=tuple(outs),
        in_specs=specs,
        out_specs=tuple([pl.BlockSpec(memory_space=pltpu.VMEM)] * len(outs)),
        scratch_shapes=list(scratch),
        compiler_params=pltpu.CompilerParams(vmem_limit_bytes=limit * MIB),
        cost_estimate=pl.CostEstimate(flops=flops, bytes_accessed=size, transcendentals=0),
    )(*operands)


def math_size(array):
    total = jnp.dtype(array.dtype).itemsize
    for d in array.shape:
        total *= d
    return total


def dot(a, b, ca, cb):
    return lax.dot_general(a, b, (((ca,), (cb,)), ((), ())), preferred_element_type=f32)


def rms_factor(wide):
    return lax.rsqrt(jnp.mean(wide * wide, axis=-1, keepdims=True) + norm_eps)


def gelu_parts(pre):
    square = pre * pre
    tangent = jnp.tanh(pre * (gelu_coef + (gelu_coef * gelu_cubic) * square))
    gate = 0.5 + 0.5 * tangent
    value = pre * gate
    slope = gate + value * (1.0 - tangent) * (gelu_coef + (3.0 * gelu_coef * gelu_cubic) * square)
    return value, slope


def first_half(flags, rows, gain, w_in, w_out, normed_back, hidden, hidden_back, grad_pre, normed):
    row = gain[...]
    x = rows[0].astype(f32)
    normed[:HALF] = (x * rms_factor(x) * row).astype(bf16)
    x = jnp.where(flags[1] == 1, x, rows[2].astype(f32))
    value = (x * rms_factor(x) * row).astype(bf16)
    normed[HALF:] = value
    normed_back[...] = value
    for cols in CHUNKS:
        pre = dot(normed[...], w_in[:, cols], 1, 0)
        value, _ = gelu_parts(pre[:HALF])
        hidden[:, cols] = value.astype(bf16)
        value, slope = gelu_parts(pre[HALF:])
        hidden_back[:, cols] = value.astype(bf16)
        grad_pre[:, cols] = (dot(rows[1], w_out[cols, :], 1, 1) * slope).astype(bf16)


def near_body(flags, near, gain, w_in, w_out, *refs):
    first_half(flags, near, gain, w_in, w_out, *refs)


def far_body(
    flags, far, gain, w_in, w_out, gain_was, *refs
):
    normed_back, hidden_back, grad_pre, send, gain_sum, hidden, normed = refs[-7:]
    first_half(flags, far, gain, w_in, w_out, normed_back, hidden, hidden_back, grad_pre, normed)
    for cols in CHUNKS:
        send[0, :, cols] = dot(hidden[...], w_out[:, cols], 1, 0).astype(bf16)
        part = dot(grad_pre[...], w_in[cols, :], 1, 1)
        send[1, :, cols] = part.astype(bf16)
        gain_sum[0, :, cols] = gain_was[0, :, cols] + gain_term(part, normed_back[:, cols])


def gain_term(part, normed):
    return jnp.sum((part * normed.astype(f32)).reshape(-1, 8, part.shape[-1]), axis=0)


def end_body(hidden_near, grad_pre, normed_back, w_in, w_out, gain_was, keep, gain_sum):
    for cols in CHUNKS:
        keep[0, :, cols] = dot(hidden_near[...], w_out[:, cols], 1, 0)
        part = dot(grad_pre[...], w_in[cols, :], 1, 1)
        keep[1, :, cols] = part
        gain_sum[0, :, cols] = gain_was[0, :, cols] + gain_term(part, normed_back[:, cols])


def split_body(keep, arrived, total, *blocks):
    for j in range(Y):
        rows = slice(j * NEAR, (j + 1) * NEAR)
        value = keep[:, rows] + arrived[:, rows].astype(f32)
        if j == 0:
            total[...] = value
        else:
            blocks[j - 1][...] = value.astype(bf16)


def stack_z(parts):
    return jnp.concatenate([p.astype(f32) for p in parts], axis=-2).astype(bf16)


def sum_body(passed, total, *refs):
    value = total[...]
    for r in refs[: Y - 1]:
        value = value + r[...].astype(f32)
    given, outs = refs[Y - 1 : Y - 1 + passed], refs[Y - 1 + passed :]
    outs[0][...] = value
    outs[1][...] = value[0].astype(bf16)
    outs[2][...] = value[1].astype(bf16)
    if passed:
        value = stack_z([r[...] for r in given])
        for i, ref in enumerate(outs[3:]):
            ref[...] = value[i]


def swap_one(rows):
    rows = [rows[i * OWN : (i + 1) * OWN] for i in range(Z)]
    return jnp.concatenate([rows[1], rows[0], rows[3], rows[2]], axis=0)


def swap_three(rows):
    return jnp.concatenate([rows[2 * OWN :], rows[: 2 * OWN]], axis=0)


def middle_body(total, fwd_in, bwd_in, ahead, summed, fwd_out, bwd_out, ahead_out):
    fwd = total[0] + swap_one(fwd_in[...].astype(f32))
    bwd = total[1] + swap_three(bwd_in[...].astype(f32))
    summed[0] = fwd
    summed[1] = bwd
    fwd_out[...] = fwd.astype(bf16)
    bwd_out[...] = bwd.astype(bf16)
    ahead_out[...] = ahead[...]


def norm_backward(x, grad_normed, grad_rows, row):
    factor = rms_factor(x)
    weighted = row * grad_normed
    inner = jnp.mean(weighted * x, axis=-1, keepdims=True)
    return grad_rows + factor * weighted - x * (factor * factor * factor) * inner


def finish_body(flags, total, fwd_in, bwd_in, near, gain, y_now, grad_x):
    fwd = total[0] + swap_three(fwd_in[...].astype(f32))
    bwd = total[1] + swap_one(bwd_in[...].astype(f32))
    x = near[0, :NEAR].astype(f32)
    y_now[...] = (x + fwd).astype(bf16)
    x_back = jnp.where(flags[1] == 1, x, near[2, :NEAR].astype(f32))
    grads = near[1, :NEAR].astype(f32)
    grad_x[...] = norm_backward(x_back, bwd, grads, gain[...]).astype(bf16)


def join_body(*refs):
    for j, part in enumerate(refs[:Y]):
        refs[-1][:, j * NEAR : (j + 1) * NEAR, :] = part[...]


def join_z_body(one, two, *refs):
    refs[-1][...] = stack_z([one[...], two[...]])


def hold_body(value, _, same):
    same[...] = value[...]


def select_body(flags, y_in, g_in, entering, *refs):
    rows = refs[-1]
    own = entering[...].astype(f32)
    rows[0] = jnp.where(flags[0] == 1, own, y_in[...].astype(f32)).astype(bf16)
    rows[1] = jnp.where(flags[1] == 1, own, g_in[...].astype(f32)).astype(bf16)


def enter_body(*refs):
    for j in range(Y):
        block = slice(j * NEAR, (j + 1) * NEAR)
        refs[-1][:2, block] = refs[j][...]
        refs[-1][2, block] = refs[Y + j][...]


def hold(value, until):
    return local(hold_body, [out(value.dtype, *value.shape)], value, until)[0]


def gather_y(rows):
    return [rows] + [route(rows, 0, -j, 0) for j in range(1, Y)]


def last_split_body(keep, arrived, gain_sum, gain_in, total, gain_total, *blocks):
    gain_value = gain_sum[...] + gain_in[...].astype(f32)
    gain_total[...] = gain_value
    for j in range(Y):
        rows = slice(j * NEAR, (j + 1) * NEAR)
        value = keep[:, rows] + arrived[:, rows].astype(f32)
        if j == 0:
            total[...] = value
        else:
            for i in range(2):
                for k in range(Z):
                    blocks[j - 1][i * Z + k] = value[i, k * OWN : (k + 1) * OWN].astype(bf16)
            blocks[j - 1][2 * Z] = gain_value[0].astype(bf16)


def last_sum_body(total, gain_total, r1, r2, r3, _, own, block):
    gain_value = gain_total[0]
    for ref in (r1, r2, r3):
        gain_value = gain_value + ref[2 * Z].astype(f32)
    for k in range(Z):
        for i in range(2):
            value = total[i, k * OWN : (k + 1) * OWN]
            for ref in (r1, r2, r3):
                value = value + ref[i * Z + k].astype(f32)
            if k < 2:
                own[2 * k + i] = value
            else:
                block[2 * (k - 2) + i] = value.astype(bf16)
    own[4] = gain_value
    block[4] = gain_value.astype(bf16)


def last_middle_body(own, got, _, summed, block):
    for i in range(2):
        summed[i] = own[i] + got[i].astype(f32)
        block[i] = (own[2 + i] + got[2 + i].astype(f32)).astype(bf16)
    value = own[4] + got[4].astype(f32)
    summed[2] = value
    block[2] = value.astype(bf16)


def last_body(flags, own, got, near, gain, *refs):
    before, (y_all, grad_all, gain_total) = refs[:-3], refs[-3:]
    for t in range(len(before) // 2):
        y_all[t] = before[2 * t][:16].astype(f32)[:OWN].astype(bf16)
        grad_all[t] = before[2 * t + 1][:16].astype(f32)[:OWN].astype(bf16)
    fwd, bwd, gain_value = (own[i] + got[i].astype(f32) for i in range(3))
    x = near[0, :16].astype(f32)[:OWN]
    y_all[len(before) // 2] = (x + fwd).astype(bf16)
    x_back = jnp.where(flags[1] == 1, x, near[2, :16].astype(f32)[:OWN])
    grads = near[1, :16].astype(f32)[:OWN]
    grad_all[len(before) // 2] = norm_backward(x_back, bwd, grads, gain[...]).astype(bf16)
    gain_total[...] = jnp.sum(gain_value, axis=0, keepdims=True) / gain[...]


def on_device(
    novel_batch_seq,
    transit_activity,
    saved_prior_entries,
    waiting_loss_slope,
    loss_slope_seq,
    norm_scaling,
    entering_matrix,
    leaving_matrix,
):
    section_pos = lax.axis_index("section")
    section_count = lax.axis_size("section")
    ticks = novel_batch_seq.shape[0]
    depth = saved_prior_entries.shape[1]
    weight_in = entering_matrix[0]
    weight_out = leaving_matrix[0]
    is_first = section_pos == 0
    is_last = section_pos == section_count - 1
    flags = jnp.stack([is_first, is_last]).astype(jnp.int32)
    x_first = jnp.where(is_first, novel_batch_seq[0], transit_activity[0])
    g_first = jnp.where(is_last, loss_slope_seq[0], waiting_loss_slope[0])
    stored = []
    for tick in range(ticks):
        index = tick + 2 * section_pos
        held = lax.dynamic_index_in_dim(
            saved_prior_entries[0], jnp.minimum(index, depth - 1), 0, keepdims=False
        )
        stored.append(jnp.where(index < depth, held, x_first))
    entering = [jnp.where(is_last, loss_slope_seq[t], novel_batch_seq[t]) for t in range(1, ticks)]
    begin = jnp.stack([x_first, g_first, stored[0]])
    later = jnp.stack(stored[1:] + entering)

    (rows,) = local(join_z_body, [out(bf16, 3, 2 * OWN, WIDE)], begin, route(begin, 1, 0, 0))
    (rows,) = local(join_z_body, [out(bf16, 3, NEAR, WIDE)], rows, route(rows, 3, 0, 0))
    parts = gather_y(rows)
    later = hold(later, parts[1])
    beside = route(later, 1, 0, 0)
    (near,) = local(join_body, [out(bf16, 3, HALF, WIDE)], *parts)
    until = [beside]
    (later,) = local(join_z_body, [out(bf16, 4, 2 * OWN, WIDE)], later, beside)
    passed = [later, route(later, 3, 0, 0)]

    block = (2, NEAR, WIDE)
    whole, half = (2 * HALF, WIDE), (HALF, WIDE)
    flops = 2 * HALF * WIDE * WIDE
    gain_sum = jnp.zeros((1, 8, WIDE), f32)
    ended, kept = [], []
    for tick in range(ticks):
        first, final = tick == 0, tick + 1 == ticks
        far = route(near, 0, 0, 1)
        back_near, hidden_near, hidden_back_near, pre_near = local(
            near_body, [out(bf16, *half)] * 4,
            flags, near, norm_scaling, weight_in, weight_out,
            scalars=1, limit=24, flops=3 * flops, scratch=[pltpu.VMEM(whole, bf16)],
        )
        back_far, hidden_back_far, pre_far, send, gain_sum = local(
            far_body, [out(bf16, *half)] * 3 + [out(bf16, 2, HALF, WIDE), out(f32, 1, 8, WIDE)],
            flags, far, norm_scaling, weight_in, weight_out, gain_sum, hidden_near, *until,
            scalars=1, limit=24, flops=5 * flops,
            scratch=[pltpu.VMEM(half, bf16), pltpu.VMEM(whole, bf16)],
        )
        until = []
        kept.append(
            [(back_near, back_far), (pre_near, pre_far), (hidden_back_near, hidden_back_far), (near[1], far[1])]
        )
        arrived = route(send, 0, 0, 1)
        keep, gain_sum = local(
            end_body, [out(f32, 2, HALF, WIDE), out(f32, 1, 8, WIDE)],
            hidden_near, pre_near, back_near, weight_in, weight_out, gain_sum,
            limit=24, flops=2 * flops,
        )
        if final:
            gain_in = route(gain_sum.astype(bf16), 0, 0, 1)
            last = (2 * Z + 1, OWN, WIDE)
            total, gain_sum, *blocks = local(
                last_split_body,
                [out(f32, *block), out(f32, 1, 8, WIDE)] + [out(bf16, *last)] * (Y - 1),
                keep, arrived, gain_sum, gain_in,
            )
            got = [route(b, 0, j + 1, 0) for j, b in enumerate(blocks)]
            kept[-1][3] = (near[1], hold(far[1], got[0]))
            normed_seq, grad_pre_seq, hidden_seq, slope_seq = (
                jnp.concatenate([rows for k in kept for rows in k[i]], axis=0) for i in range(4)
            )
            grad_out = dot(hidden_seq, slope_seq, 0, 0).astype(bf16)
            own, block = local(
                last_sum_body, [out(f32, 5, OWN, WIDE), out(bf16, 5, OWN, WIDE)],
                total, gain_sum, *got, grad_out, loose=1,
            )
            grad_in = dot(normed_seq, grad_pre_seq, 0, 0).astype(bf16)
            own, block = local(
                last_middle_body, [out(f32, 3, OWN, WIDE), out(bf16, 3, OWN, WIDE)],
                own, route(block, 3, 0, 0), grad_in, loose=1,
            )
            got = route(block, 1, 0, 0)
            forward_out, backward_out, gain_total = local(
                last_body,
                [out(bf16, ticks, OWN, WIDE), out(bf16, ticks, OWN, WIDE), out(f32, 1, WIDE)],
                flags, own, got, near, norm_scaling, *ended, scalars=1,
            )
            break
        total, *blocks = local(
            split_body, [out(f32, *block)] + [out(bf16, *block)] * (Y - 1), keep, arrived
        )
        got = [route(b, 0, j + 1, 0) for j, b in enumerate(blocks)]
        total, fwd, bwd, *rest = local(
            functools.partial(sum_body, len(passed)),
            [out(f32, *block)] + [out(bf16, NEAR, WIDE)] * (6 if first else 2),
            total, *got, *passed,
        )
        if first:
            ahead, entering, passed = rest[:2], rest[2:], []
        total, fwd, bwd, beside = local(
            middle_body,
            [out(f32, *block)] + [out(bf16, NEAR, WIDE)] * 3,
            total, route(fwd, 1, 0, 0), route(bwd, 3, 0, 0), ahead[tick],
        )
        beside = gather_y(beside)
        y_now, grad_x = local(
            finish_body, [out(bf16, NEAR, WIDE)] * 2,
            flags, total, route(fwd, 3, 0, 0), route(bwd, 1, 0, 0), near, norm_scaling, scalars=1,
        )
        ended += [y_now, grad_x]
        y_in, g_in = shifted(y_now, 1), shifted(grad_x, -1)
        (rows,) = local(
            select_body, [out(bf16, *block)], flags, y_in, g_in, entering[tick], *beside,
            scalars=1,
        )
        (near,) = local(enter_body, [out(bf16, 3, HALF, WIDE)], *gather_y(rows), *beside)

    return (
        forward_out[None],
        backward_out[None],
        grad_in[None],
        grad_out[None],
        gain_total,
    )


def solution(mesh):
    placed = (
        P(None, "dp", None),
        P("section", "dp", None),
        P("section", None, "dp", None),
        P("section", "dp", None),
        P(None, "dp", None),
        P("section", None),
        P("section", None, "dp"),
        P("section", "dp", None),
    )
    return jax.shard_map(
        on_device,
        mesh=mesh,
        in_specs=placed,
        out_specs=(
            P("section", None, "dp", None),
            P("section", None, "dp", None),
            P("section", None, "dp"),
            P("section", "dp", None),
            P("section", None),
        ),
        check_vma=False,
    )
```
